512 devices in a mesh: seq: 32 (over x, y), ch: 16 (over z, core).
Axes of the slice: x: 4, y: 8, z: 8, core: 2. Of those that a mesh axis runs over, the one named last changes fastest.
Arguments:
- first_gate: bfloat16 [8192, 4096], P('seq', 'ch'), parts along dimension 1, may hold values from -6 to 6
- second_gate: bfloat16 [8192, 4096], P('seq', 'ch'), parts along dimension 1, may hold values from -6 to 6
- values_in: bfloat16 [8192, 4096], P('seq', 'ch'), parts along dimension 1, may hold values from -6 to 6
- cotangent: bfloat16 [8192, 4096], P('seq', 'ch'), parts along dimension 1, may hold values from -6 to 6
- filters: bfloat16 [131072], P(('ch', 'seq')), parts along dimension 0, may hold values from -0.0625 to 0.0625
- skip_gain: float32 [4096], P('ch'), parts along dimension 0, may hold values from -4 to 4
Outputs:
- output: bfloat16 [8192, 4096], P('seq', 'ch'), parts along dimension 1
- grad_first: bfloat16 [8192, 4096], P('seq', 'ch'), parts along dimension 1
- grad_second: bfloat16 [8192, 4096], P('seq', 'ch'), parts along dimension 1
- grad_values: bfloat16 [8192, 4096], P('seq', 'ch'), parts along dimension 1
The draws below stay inside these ranges and needn't reach their ends.
There are 16 independent parts, one for each index of `ch`. The reference program is written for one: setup_inputs(seed, part) draws one part's arguments, and reference() takes and returns one part's arrays. A program takes and returns all parts, laid end to end along the dimension named above; each array names one. Nothing has to cross between parts.
All inputs are finite; a program needn't handle non-finite values.
Results may differ from the reference program's by a relative error of at most 0.0049.
Values may be sent and summed in bfloat16 or wider, within the bound.
A program may use at most 64 MiB of HBM per device.

```python
import jax
import jax.numpy as jnp
import numpy as np

CH = 256
BLOCK = 128
BLOCKS = 64
SEQ = 8192


def level_of(own_key, extent, shards, least, largest):
    factor_of = 1.0
    for position, blocks in shards:
        draws = jax.random.uniform(jax.random.fold_in(jax.random.fold_in(own_key, 6), position), (blocks,), jnp.float32, least / len(shards), largest / len(shards))
        factor_of = factor_of * jnp.repeat(jnp.exp(draws), extent[position] // blocks).reshape((-1,) + (1,) * (len(extent) - 1 - position))
    return factor_of


def gaussian(key, dims, spread, bound, split=(), dtype=jnp.bfloat16):
    factor_of = level_of(key, dims, split, -0.22, 0.18) if split else 1.0
    values = jax.random.normal(key, dims, jnp.float32) * spread * factor_of
    return jnp.minimum(jnp.maximum(values, -bound), bound).astype(dtype)


def setup_inputs(seed: int = 0, part: int = 0) -> dict:
    arg_keys = jax.random.split(jax.random.key(seed), 7)
    part_splits = jax.random.split(jax.random.fold_in(arg_keys[6], part), 7)
    return {
        "first_gate": gaussian(part_splits[0], (SEQ, CH), 1.0, 6.0, ((0, 32),)),
        "second_gate": gaussian(part_splits[1], (SEQ, CH), 1.0, 6.0, ((0, 32),)),
        "values_in": gaussian(part_splits[2], (SEQ, CH), 1.0, 6.0, ((0, 32),)),
        "cotangent": gaussian(part_splits[3], (SEQ, CH), 1.0, 6.0, ((0, 32),)),
        "filters": gaussian(part_splits[4], (SEQ,), SEQ ** -0.5, 0.0625, ((0, 32),)),
        "skip_gain": gaussian(part_splits[5], (CH,), 1.0, 4.0, (), jnp.float32),
    }


def time_order(blocks_count):
    half = blocks_count // 2
    return [2 * t if t < half else 2 * (blocks_count - 1 - t) + 1 for t in range(blocks_count)]


def causal_conv(spectrum, signal):
    length = signal.shape[0]
    transformed = jnp.fft.rfft(signal, n=2 * length, axis=0)
    return jnp.fft.irfft(spectrum[:, None] * transformed, n=2 * length, axis=0)[:length]


def reference(first_gate, second_gate, values_in, cotangent, filters, skip_gain):
    order = np.array(time_order(BLOCKS))
    inverse = np.argsort(order)

    def to_time(field):
        return field.reshape(BLOCKS, BLOCK, CH)[order].reshape(SEQ, CH)

    def to_storage(field):
        return field.reshape(BLOCKS, BLOCK, CH)[inverse].reshape(SEQ, CH)

    first_f = to_time(first_gate).astype(jnp.float32)
    second_f = to_time(second_gate).astype(jnp.float32)
    values_f = to_time(values_in).astype(jnp.float32)
    cotan_f = to_time(cotangent).astype(jnp.float32)
    gated_product = (first_f * second_f).astype(jnp.bfloat16).astype(jnp.float32)
    carried = (cotan_f * values_f).astype(jnp.bfloat16).astype(jnp.float32)
    spectrum = jnp.fft.rfft(filters.astype(jnp.float32), n=2 * SEQ)
    longconv = causal_conv(spectrum, gated_product)
    backconv = causal_conv(spectrum, carried[::-1])[::-1]
    skip_scale = skip_gain.astype(jnp.float32)[None, :]
    mixed_total = longconv + skip_scale * gated_product
    output = (values_f * mixed_total).astype(jnp.bfloat16)
    grad_mixed = backconv + skip_scale * carried
    grad_first = (grad_mixed * second_f).astype(jnp.bfloat16)
    grad_second = (grad_mixed * first_f).astype(jnp.bfloat16)
    grad_values = (cotan_f * mixed_total).astype(jnp.bfloat16)
    return (to_storage(output), to_storage(grad_first), to_storage(grad_second), to_storage(grad_values))
```

```python
import functools

import jax
import jax.numpy as jnp
from jax import lax
from jax.experimental import pallas as pl
from jax.experimental.pallas import tpu as pltpu
from jax.sharding import PartitionSpec as P

BF16 = jnp.bfloat16
F32 = jnp.float32
SUB = 8
ROWS = 2 * SUB
NT = (((1,), (1,)), ((), ()))


def select_matrix(size, flipped):
    row = lax.broadcasted_iota(jnp.int32, (size, size), 0)
    col = lax.broadcasted_iota(jnp.int32, (size, size), 1)
    hit = (row + col == size - 1) if flipped else (row == col)
    return jnp.where(hit, 1.0, 0.0).astype(BF16)


def kernel(
    n,
    fg_hbm, sg_hbm, vi_hbm, ct_hbm, taps_ref, skip_ref,
    fwd_ref, bwd_ref,
    fields, tap_buf, send1, recv1, xbuf, slab, acc, send2, recv2,
    in_sem, tap_send, tap_recv, send1_sem, recv1_sem, send2_sem, recv2_sem,
):
    me = lax.axis_index("seq")
    half = fg_hbm.shape[0] // 2
    chunk = 2 * half
    channels = fg_hbm.shape[1]

    def each_peer(visit):
        def body(k, carry):
            visit(lax.rem(me + k, n))
            return carry
        lax.fori_loop(1, n, body, 0)

    loads = [
        pltpu.make_async_copy(src, fields.at[k], in_sem.at[k])
        for k, src in enumerate((fg_hbm, sg_hbm, ct_hbm, vi_hbm))
    ]
    for load in loads:
        load.start()
    barrier = pltpu.get_barrier_semaphore()
    each_peer(lambda peer: pl.semaphore_signal(barrier, inc=1, device_id={"seq": peer}))

    tap_buf[0] = jnp.zeros((1, chunk), F32)
    tap_buf[me + 1] = taps_ref[...]

    plain = select_matrix(chunk, False)
    flipped = select_matrix(chunk, True)
    loads[0].wait()
    loads[1].wait()
    gated = (fields[0].astype(F32) * fields[1].astype(F32)).astype(BF16)
    across = plain if channels == chunk else select_matrix(channels, False)
    gated_t = lax.dot_general(across, gated, NT, preferred_element_type=F32)
    loads[2].wait()
    loads[3].wait()
    carried = (fields[2].astype(F32) * fields[3].astype(F32)).astype(BF16)
    carried_r = jnp.dot(flipped, carried, preferred_element_type=F32).astype(BF16)
    carried_t = lax.dot_general(across, carried_r, NT, preferred_element_type=F32)
    both = jnp.concatenate(
        [gated_t.reshape(n, SUB, chunk), carried_t.reshape(n, SUB, chunk)], axis=1
    )
    send1[...] = both.astype(BF16)
    recv1[me] = send1[me]

    pl.semaphore_wait(barrier, n - 1)

    def send_taps(peer):
        pltpu.make_async_remote_copy(
            src_ref=taps_ref, dst_ref=tap_buf.at[me + 1],
            send_sem=tap_send, recv_sem=tap_recv, device_id={"seq": peer},
        ).start()

    def send_first(peer):
        pltpu.make_async_remote_copy(
            src_ref=send1.at[peer], dst_ref=recv1.at[me],
            send_sem=send1_sem, recv_sem=recv1_sem, device_id={"seq": peer},
        ).start()

    def send_second(peer):
        pltpu.make_async_remote_copy(
            src_ref=send2.at[peer], dst_ref=recv2.at[me],
            send_sem=send2_sem, recv_sem=recv2_sem, device_id={"seq": peer},
        ).start()

    def whole(buf, send_sem, recv_sem):
        part = buf.at[pl.ds(0, n - 1)]
        return pltpu.make_async_remote_copy(
            src_ref=part, dst_ref=part, send_sem=send_sem, recv_sem=recv_sem,
            device_id={"seq": lax.rem(me + 1, n)},
        )

    each_peer(send_taps)
    each_peer(send_first)

    all_taps = whole(tap_buf, tap_send, tap_recv)
    all_taps.wait_recv()
    slab[:, 0:half] = jnp.zeros((half, half), BF16)

    def build(j, carry):
        window = jnp.concatenate([tap_buf[j][:, half:], tap_buf[j + 1]], axis=1)
        window = jnp.broadcast_to(window, (ROWS, half + chunk))
        skewed = pltpu.roll(window, 0, 1, stride=1, stride_axis=0)
        for k in range(half // ROWS):
            moved = skewed if k == 0 else pltpu.roll(skewed, k * ROWS, 1)
            slab[k * ROWS:(k + 1) * ROWS, pl.ds(pl.multiple_of(j * chunk + half, half), chunk)] = (
                moved[:, half:].astype(BF16)
            )
        return carry

    lax.fori_loop(0, n, build, 0)

    lane = lax.broadcasted_iota(jnp.int32, (ROWS, channels), 1)
    row = lax.broadcasted_iota(jnp.int32, (ROWS, channels), 0)
    mine = lane == me * SUB + lax.rem(row, SUB)
    gains = jnp.sum(jnp.where(mine, skip_ref[...], 0.0), axis=1, keepdims=True)

    first = whole(recv1, send1_sem, recv1_sem)
    first.wait_recv()
    for block in range(2 * n):
        source, side = (block, 0) if block < n else (2 * n - 1 - block, 1)
        piece = recv1[source, :, side * half:(side + 1) * half]
        pair, place = block // 2, block % 2
        at = (slice(pair * ROWS, (pair + 1) * ROWS), slice(place * half, (place + 1) * half))
        xbuf[at] = piece
        acc[at] = gains * piece.astype(F32)

    total = n * ROWS
    groups = 4
    per = n // groups
    for g in range(groups):
        depth = total - g * per * ROWS

        def step(d, carry):
            top = slab[:, pl.ds(pl.multiple_of(d * chunk + half, half), chunk)]
            low = slab[:, pl.ds(pl.multiple_of(d * chunk, chunk), chunk)]
            lags = jnp.concatenate([top, low], axis=0)
            term = jnp.dot(xbuf[0:depth, :], lags, preferred_element_type=F32)
            rows = pl.ds(pl.multiple_of(d * ROWS, ROWS), depth)
            acc[rows, :] = acc[rows, :] + term
            return carry

        lax.fori_loop(g * per, (g + 1) * per, step, 0)

    for dst in range(n):
        left, right = dst, 2 * n - 1 - dst
        pieces = [
            acc[(b // 2) * ROWS:(b // 2 + 1) * ROWS, (b % 2) * half:(b % 2 + 1) * half]
            for b in (left, right)
        ]
        send2[dst] = jnp.concatenate(pieces, axis=1).astype(BF16)
    recv2[me] = send2[me]
    each_peer(send_second)
    second = whole(recv2, send2_sem, recv2_sem)
    second.wait_recv()
    back = recv2[...].astype(F32)
    fwd_t = back[:, 0:SUB, :].reshape(channels, chunk).astype(BF16)
    bwd_t = back[:, SUB:, :].reshape(channels, chunk).astype(BF16)
    fwd_ref[...] = lax.dot_general(plain, fwd_t, NT, preferred_element_type=F32).astype(BF16)
    bwd_ref[...] = lax.dot_general(flipped, bwd_t, NT, preferred_element_type=F32).astype(BF16)
    all_taps.wait_send()
    first.wait_send()
    second.wait_send()


def on_device(n, first_gate, second_gate, values_in, cotangent, filters, skip_gain):
    chunk, channels = first_gate.shape
    half = chunk // 2
    taps = filters.astype(F32).reshape(1, chunk)
    anywhere = pl.BlockSpec(memory_space=pl.ANY)
    in_vmem = pl.BlockSpec(memory_space=pltpu.VMEM)
    result = jax.ShapeDtypeStruct((chunk, channels), BF16)
    message = pltpu.VMEM((n, ROWS, chunk), BF16)
    mixed_total, grad_mixed = pl.pallas_call(
        functools.partial(kernel, n),
        out_shape=(result, result),
        in_specs=[anywhere] * 4 + [in_vmem] * 2,
        out_specs=(in_vmem, in_vmem),
        scratch_shapes=[
            pltpu.VMEM((4, chunk, channels), BF16),
            pltpu.VMEM((n + 1, 1, chunk), F32),
            message,
            message,
            pltpu.VMEM((n * ROWS, chunk), BF16),
            pltpu.VMEM((half, half + n * chunk), BF16),
            pltpu.VMEM((n * ROWS + n * ROWS // 4, chunk), F32),
            message,
            message,
            pltpu.SemaphoreType.DMA((4,)),
            pltpu.SemaphoreType.DMA,
            pltpu.SemaphoreType.DMA,
            pltpu.SemaphoreType.DMA,
            pltpu.SemaphoreType.DMA,
            pltpu.SemaphoreType.DMA,
            pltpu.SemaphoreType.DMA,
        ],
        compiler_params=pltpu.CompilerParams(
            collective_id=0, has_side_effects=True, vmem_limit_bytes=32 * 1024 * 1024
        ),
    )(first_gate, second_gate, values_in, cotangent, taps, skip_gain.reshape(1, channels))
    mixed_total = mixed_total.astype(F32)
    grad_mixed = grad_mixed.astype(F32)
    output = (values_in.astype(F32) * mixed_total).astype(BF16)
    grad_first = (grad_mixed * second_gate.astype(F32)).astype(BF16)
    grad_second = (grad_mixed * first_gate.astype(F32)).astype(BF16)
    grad_values = (cotangent.astype(F32) * mixed_total).astype(BF16)
    return (output, grad_first, grad_second, grad_values)


def solution(mesh):
    rows = P("seq", "ch")
    return jax.shard_map(
        functools.partial(on_device, mesh.shape["seq"]),
        mesh=mesh,
        in_specs=(rows, rows, rows, rows, P(("ch", "seq")), P("ch")),
        out_specs=(rows, rows, rows, rows),
        check_vma=False,
    )
```

```python
import functools

import jax
import jax.numpy as jnp
from jax import lax
from jax.experimental import pallas as pl
from jax.experimental.pallas import tpu as pltpu
from jax.sharding import PartitionSpec as P

BF16 = jnp.bfloat16
F32 = jnp.float32
SUB = 8
ROWS = 2 * SUB
NT = (((1,), (1,)), ((), ()))


def select_matrix(size, flipped):
    row = lax.broadcasted_iota(jnp.int32, (size, size), 0)
    col = lax.broadcasted_iota(jnp.int32, (size, size), 1)
    hit = (row + col == size - 1) if flipped else (row == col)
    return jnp.where(hit, 1.0, 0.0).astype(BF16)


def kernel(
    n,
    fg_hbm, sg_hbm, vi_hbm, ct_hbm, taps_hbm, skip_hbm,
    fwd_ref, bwd_ref, fg, sg, vi, ct,
    tap_own, skip_own, tap_buf, send1, recv1, xbuf, slab, acc, send2, recv2,
    in_sem, tap_send, tap_recv, send1_sem, recv1_sem, send2_sem, recv2_sem,
):
    me = lax.axis_index("seq")
    half = fg_hbm.shape[0] // 2
    chunk = 2 * half
    channels = fg_hbm.shape[1]

    def each_peer(visit):
        def body(k, carry):
            visit(lax.rem(me + k, n))
            return carry
        lax.fori_loop(1, n, body, 0)

    barrier = pltpu.get_barrier_semaphore()
    each_peer(lambda peer: pl.semaphore_signal(barrier, inc=1, device_id={"seq": peer}))
    loads = [
        pltpu.make_async_copy(src, dst, in_sem.at[k])
        for k, (src, dst) in enumerate(
            ((taps_hbm, tap_own), (fg_hbm, fg), (sg_hbm, sg), (ct_hbm, ct), (vi_hbm, vi), (skip_hbm, skip_own))
        )
    ]
    for load in loads:
        load.start()

    tap_buf[0] = jnp.zeros((1, chunk), F32)
    loads[0].wait()
    own = tap_own[...].astype(F32)
    tap_buf[me + 1] = jnp.concatenate([own[0:1], own[1:2]], axis=1)

    plain = select_matrix(chunk, False)
    flipped = select_matrix(chunk, True)
    loads[1].wait()
    loads[2].wait()
    gated = (fg[...].astype(F32) * sg[...].astype(F32)).astype(BF16)
    across = plain if channels == chunk else select_matrix(channels, False)
    gated_t = lax.dot_general(across, gated, NT, preferred_element_type=F32)
    loads[3].wait()
    loads[4].wait()
    carried = (ct[...].astype(F32) * vi[...].astype(F32)).astype(BF16)
    carried_r = jnp.dot(flipped, carried, preferred_element_type=F32).astype(BF16)
    carried_t = lax.dot_general(across, carried_r, NT, preferred_element_type=F32)
    both = jnp.concatenate(
        [gated_t.reshape(n, SUB, chunk), carried_t.reshape(n, SUB, chunk)], axis=1
    )
    send1[...] = both.astype(BF16)
    recv1[me] = send1[me]

    pl.semaphore_wait(barrier, n - 1)

    def send_taps(peer):
        pltpu.make_async_remote_copy(
            src_ref=tap_buf.at[me + 1], dst_ref=tap_buf.at[me + 1],
            send_sem=tap_send, recv_sem=tap_recv, device_id={"seq": peer},
        ).start()

    def send_first(peer):
        pltpu.make_async_remote_copy(
            src_ref=send1.at[peer], dst_ref=recv1.at[me],
            send_sem=send1_sem, recv_sem=recv1_sem, device_id={"seq": peer},
        ).start()

    def send_second(peer):
        pltpu.make_async_remote_copy(
            src_ref=send2.at[peer], dst_ref=recv2.at[me],
            send_sem=send2_sem, recv_sem=recv2_sem, device_id={"seq": peer},
        ).start()

    def whole(buf, send_sem, recv_sem):
        part = buf.at[pl.ds(0, n - 1)]
        return pltpu.make_async_remote_copy(
            src_ref=part, dst_ref=part, send_sem=send_sem, recv_sem=recv_sem,
            device_id={"seq": lax.rem(me + 1, n)},
        )

    each_peer(send_taps)
    each_peer(send_first)

    all_taps = whole(tap_buf, tap_send, tap_recv)
    all_taps.wait_recv()
    slab[:, 0:half] = jnp.zeros((half, half), BF16)

    def build(j, carry):
        window = jnp.concatenate([tap_buf[j][:, half:], tap_buf[j + 1]], axis=1)
        window = jnp.broadcast_to(window, (half, half + chunk))
        skewed = pltpu.roll(window, 0, 1, stride=1, stride_axis=0)
        slab[:, pl.ds(pl.multiple_of(j * chunk + half, half), chunk)] = skewed[:, half:].astype(BF16)
        return carry

    lax.fori_loop(0, n, build, 0, unroll=4)

    lane = lax.broadcasted_iota(jnp.int32, (ROWS, channels), 1)
    row = lax.broadcasted_iota(jnp.int32, (ROWS, channels), 0)
    mine = lane == me * SUB + lax.rem(row, SUB)
    loads[5].wait()
    gains = jnp.sum(jnp.where(mine, skip_own[...], 0.0), axis=1, keepdims=True)

    first = whole(recv1, send1_sem, recv1_sem)
    first.wait_recv()
    for block in range(2 * n):
        source, side = (block, 0) if block < n else (2 * n - 1 - block, 1)
        piece = recv1[source, :, side * half:(side + 1) * half]
        pair, place = block // 2, block % 2
        at = (slice(pair * ROWS, (pair + 1) * ROWS), slice(place * half, (place + 1) * half))
        xbuf[at] = piece
        acc[at] = gains * piece.astype(F32)

    total = n * ROWS
    for d in range(n):
        top = slab[:, d * chunk + half:(d + 1) * chunk + half]
        low = slab[:, d * chunk:(d + 1) * chunk]
        lags = jnp.concatenate([top, low], axis=0)
        term = jnp.dot(xbuf[0:total - d * ROWS, :], lags, preferred_element_type=F32)
        acc[d * ROWS:total, :] = acc[d * ROWS:total, :] + term

    for dst in range(n):
        left, right = dst, 2 * n - 1 - dst
        pieces = [
            acc[(b // 2) * ROWS:(b // 2 + 1) * ROWS, (b % 2) * half:(b % 2 + 1) * half]
            for b in (left, right)
        ]
        send2[dst] = jnp.concatenate(pieces, axis=1).astype(BF16)
    recv2[me] = send2[me]
    each_peer(send_second)
    second = whole(recv2, send2_sem, recv2_sem)
    second.wait_recv()
    back = recv2[...].astype(F32)
    fwd_t = back[:, 0:SUB, :].reshape(channels, chunk).astype(BF16)
    bwd_t = back[:, SUB:, :].reshape(channels, chunk).astype(BF16)
    fwd_ref[...] = lax.dot_general(plain, fwd_t, NT, preferred_element_type=F32).astype(BF16)
    bwd_ref[...] = lax.dot_general(flipped, bwd_t, NT, preferred_element_type=F32).astype(BF16)
    all_taps.wait_send()
    first.wait_send()
    second.wait_send()


def on_device(n, first_gate, second_gate, values_in, cotangent, filters, skip_gain):
    chunk, channels = first_gate.shape
    half = chunk // 2
    taps = filters.reshape(2, half)
    in_hbm = pl.BlockSpec(memory_space=pltpu.HBM)
    in_vmem = pl.BlockSpec(memory_space=pltpu.VMEM)
    result = pltpu.VMEM((chunk, channels), BF16)
    message = pltpu.VMEM((n, ROWS, chunk), BF16)
    mixed_total, grad_mixed, first_gate, second_gate, values_in, cotangent = pl.pallas_call(
        functools.partial(kernel, n),
        out_shape=(result,) * 6,
        in_specs=[in_hbm] * 6,
        out_specs=(in_vmem,) * 6,
        scratch_shapes=[
            pltpu.VMEM((2, half), BF16),
            pltpu.VMEM((1, channels), F32),
            pltpu.VMEM((n + 1, 1, chunk), F32),
            message,
            message,
            pltpu.VMEM((n * ROWS, chunk), BF16),
            pltpu.VMEM((half, half + n * chunk), BF16),
            pltpu.VMEM((n * ROWS, chunk), F32),
            message,
            message,
            pltpu.SemaphoreType.DMA((6,)),
            pltpu.SemaphoreType.DMA,
            pltpu.SemaphoreType.DMA,
            pltpu.SemaphoreType.DMA,
            pltpu.SemaphoreType.DMA,
            pltpu.SemaphoreType.DMA,
            pltpu.SemaphoreType.DMA,
        ],
        compiler_params=pltpu.CompilerParams(
            collective_id=0, has_side_effects=True, vmem_limit_bytes=32 * 1024 * 1024
        ),
    )(*[
        pltpu.with_memory_space_constraint(x, pltpu.HBM)
        for x in (first_gate, second_gate, values_in, cotangent, taps, skip_gain.reshape(1, channels))
    ])
    mixed_total = mixed_total.astype(F32)
    grad_mixed = grad_mixed.astype(F32)
    output = (values_in.astype(F32) * mixed_total).astype(BF16)
    grad_first = (grad_mixed * second_gate.astype(F32)).astype(BF16)
    grad_second = (grad_mixed * first_gate.astype(F32)).astype(BF16)
    grad_values = (cotangent.astype(F32) * mixed_total).astype(BF16)
    return (output, grad_first, grad_second, grad_values)


def solution(mesh):
    rows = P("seq", "ch")
    return jax.shard_map(
        functools.partial(on_device, mesh.shape["seq"]),
        mesh=mesh,
        in_specs=(rows, rows, rows, rows, P(("ch", "seq")), P("ch")),
        out_specs=(rows, rows, rows, rows),
        check_vma=False,
    )
```

```python
import functools

import jax
import jax.numpy as jnp
from jax import lax
from jax.experimental import pallas as pl
from jax.experimental.pallas import tpu as pltpu
from jax.sharding import PartitionSpec as P

BF16 = jnp.bfloat16
F32 = jnp.float32
SUB = 8
LINES = 4
NT = (((1,), (1,)), ((), ()))


def select_matrix(size, flipped):
    row = lax.broadcasted_iota(jnp.int32, (size, size), 0)
    col = lax.broadcasted_iota(jnp.int32, (size, size), 1)
    hit = (row + col == size - 1) if flipped else (row == col)
    return jnp.where(hit, 1.0, 0.0).astype(BF16)


def ring(step, size):
    return min(step, size - step)


def far_first(n):
    size = n // LINES
    steps = [(dx, dy) for dx in range(LINES) for dy in range(size)][1:]
    return sorted(steps, key=lambda s: (-ring(s[1], size), -ring(s[0], LINES), s))


def corner_first(n):
    size = n // LINES
    return sorted(range(n), key=lambda d: (ring(d % size, size) * 2 + ring(d // size, LINES) * 2 + (d % size > size // 2), d))


def kernel(
    n,
    fg_hbm, sg_hbm, vi_hbm, ct_hbm, taps_hbm, skip_hbm,
    fwd_ref, bwd_ref, fg, sg, vi, ct,
    tap_own, skip_own, tap_buf, send1, recv1, xbuf, slab, acc, send2, recv2,
    in_sem, tap_send, tap_recv, send1_sem, recv1_sem, send2_sem, recv2_sem,
):
    me = lax.axis_index("seq")
    half = fg_hbm.shape[0] // 2
    chunk = 2 * half
    channels = fg_hbm.shape[1]
    size = n // LINES
    line, place = me // size, lax.rem(me, size)

    def each_far_first(visit):
        for dx, dy in far_first(n):
            visit(lax.rem(line + dx, LINES) * size + lax.rem(place + dy, size))

    def each_corner_first(visit):
        for peer in corner_first(n):
            @pl.when(me != peer)
            def _(peer=peer):
                visit(peer)

    barrier = pltpu.get_barrier_semaphore()
    each_far_first(lambda peer: pl.semaphore_signal(barrier, inc=1, device_id={"seq": peer}))
    loads = [
        pltpu.make_async_copy(src, dst, in_sem.at[k])
        for k, (src, dst) in enumerate(
            ((taps_hbm, tap_own), (fg_hbm, fg), (sg_hbm, sg), (ct_hbm, ct), (vi_hbm, vi), (skip_hbm, skip_own))
        )
    ]
    for load in loads:
        load.start()

    tap_buf[0] = jnp.zeros((1, chunk), F32)
    slab[:, 0:half] = jnp.zeros((half, half), BF16)
    loads[0].wait()
    own = tap_own[...].astype(F32)
    tap_buf[me + 1] = jnp.concatenate([own[0:1], own[1:2]], axis=1)

    def messages(field):
        split = field.reshape(n, SUB, chunk)
        return jnp.concatenate([split[:, :, :half], split[:, :, half:]], axis=1).astype(BF16)

    plain = select_matrix(chunk, False)
    flipped = select_matrix(chunk, True)
    across = plain if channels == chunk else select_matrix(channels, False)
    loads[1].wait()
    loads[2].wait()
    gated = (fg[...].astype(F32) * sg[...].astype(F32)).astype(BF16)
    send1[0] = messages(lax.dot_general(across, gated, NT, preferred_element_type=F32))
    loads[3].wait()
    loads[4].wait()
    carried = (ct[...].astype(F32) * vi[...].astype(F32)).astype(BF16)
    carried = jnp.dot(flipped, carried, preferred_element_type=F32).astype(BF16)
    send1[1] = messages(lax.dot_general(across, carried, NT, preferred_element_type=F32))
    for way in range(2):
        recv1[way, me] = send1[way, me]

    lane = lax.broadcasted_iota(jnp.int32, (SUB, channels), 1)
    row = lax.broadcasted_iota(jnp.int32, (SUB, channels), 0)
    loads[5].wait()
    gains = jnp.sum(jnp.where(lane == me * SUB + row, skip_own[...], 0.0), axis=1, keepdims=True)

    pl.semaphore_wait(barrier, n - 1)

    def send_taps(peer):
        pltpu.make_async_remote_copy(
            src_ref=tap_buf.at[me + 1], dst_ref=tap_buf.at[me + 1],
            send_sem=tap_send, recv_sem=tap_recv.at[line], device_id={"seq": peer},
        ).start()

    def send_first(way, peer):
        pltpu.make_async_remote_copy(
            src_ref=send1.at[way, peer], dst_ref=recv1.at[way, me],
            send_sem=send1_sem.at[way], recv_sem=recv1_sem.at[way], device_id={"seq": peer},
        ).start()

    def send_second(way, peer):
        pltpu.make_async_remote_copy(
            src_ref=send2.at[way, peer], dst_ref=recv2.at[way, me],
            send_sem=send2_sem.at[way], recv_sem=recv2_sem.at[way], device_id={"seq": peer},
        ).start()

    def several(buf, count, send_sem, recv_sem):
        part = buf.at[pl.ds(0, count)]
        return pltpu.make_async_remote_copy(
            src_ref=part, dst_ref=part, send_sem=send_sem, recv_sem=recv_sem,
            device_id={"seq": lax.rem(me + 1, n)},
        )

    each_far_first(send_taps)
    for way in range(2):
        each_far_first(functools.partial(send_first, way))

    def build(j):
        window = jnp.concatenate([tap_buf[j][:, half:], tap_buf[j + 1]], axis=1)
        window = jnp.broadcast_to(window, (half, half + chunk))
        skewed = pltpu.roll(window, 0, 1, stride=1, stride_axis=0)
        slab[:, pl.ds(pl.multiple_of(j * chunk + half, half), chunk)] = skewed[:, half:].astype(BF16)

    for dx in sorted(range(LINES), key=lambda dx: (ring(dx, LINES), dx)):
        source = lax.rem(line + dx, LINES)
        arrived = size - 1 if dx == 0 else size
        if arrived:
            several(tap_buf, arrived, tap_send, tap_recv.at[source]).wait_recv()
        for place_of in range(1, size):
            build(source * size + place_of)
    for source in range(LINES):
        build(source * size)

    for way in range(2):
        first = several(recv1.at[way], n - 1, send1_sem.at[way], recv1_sem.at[way])
        first.wait_recv()

        def block_of(block):
            source, side = (block, 0) if block < n else (2 * n - 1 - block, 1)
            return recv1[way, source].astype(F32)[side * SUB:(side + 1) * SUB]

        for pair in range(0, n, 2):
            for side in range(2):
                lanes = slice(side * half, (side + 1) * half)
                both = jnp.concatenate([block_of(2 * pair + side), block_of(2 * pair + 2 + side)], axis=0)
                xbuf[pair * SUB:(pair + 2) * SUB, lanes] = both.astype(BF16)
                acc[pair * SUB:(pair + 1) * SUB, lanes] = gains * both[:SUB]
                acc[(pair + 1) * SUB:(pair + 2) * SUB, lanes] = gains * both[SUB:]

        total = n * SUB
        for d in range(n):
            top = slab[:, d * chunk + half:(d + 1) * chunk + half]
            low = slab[:, d * chunk:(d + 1) * chunk]
            lags = jnp.concatenate([top, low], axis=0)
            depth = total - d * SUB
            padded = -(-depth // (2 * SUB)) * 2 * SUB
            term = jnp.dot(xbuf[0:padded, :], lags, preferred_element_type=F32)
            acc[d * SUB:total, :] = acc[d * SUB:total, :] + term[:depth]

        for dst in range(n):
            pieces = [
                acc[(b // 2) * SUB:(b // 2 + 1) * SUB, (b % 2) * half:(b % 2 + 1) * half]
                for b in (dst, 2 * n - 1 - dst)
            ]
            send2[way, dst] = jnp.concatenate(pieces, axis=0).astype(BF16)
        each_corner_first(functools.partial(send_second, way))
        recv2[way, me] = send2[way, me]

    for way, (out, matrix) in enumerate(((fwd_ref, plain), (bwd_ref, flipped))):
        second = several(recv2.at[way], n - 1, send2_sem.at[way], recv2_sem.at[way])
        second.wait_recv()
        back = recv2[way].astype(F32)
        left = back[:, :SUB].reshape(channels, half)
        right = back[:, SUB:].reshape(channels, half)
        back = jnp.concatenate([left, right], axis=1).astype(BF16)
        out[...] = lax.dot_general(matrix, back, NT, preferred_element_type=F32).astype(BF16)

    several(tap_buf, n - 1, tap_send, tap_recv.at[0]).wait_send()
    for way in range(2):
        several(recv1.at[way], n - 1, send1_sem.at[way], recv1_sem.at[way]).wait_send()
        several(recv2.at[way], n - 1, send2_sem.at[way], recv2_sem.at[way]).wait_send()


def on_device(n, first_gate, second_gate, values_in, cotangent, filters, skip_gain):
    chunk, channels = first_gate.shape
    half = chunk // 2
    taps = filters.reshape(2, half)
    in_hbm = pl.BlockSpec(memory_space=pltpu.HBM)
    in_vmem = pl.BlockSpec(memory_space=pltpu.VMEM)
    result = pltpu.VMEM((chunk, channels), BF16)
    message = pltpu.VMEM((2, n, 2 * SUB, half), BF16)
    mixed_total, grad_mixed, first_gate, second_gate, values_in, cotangent = pl.pallas_call(
        functools.partial(kernel, n),
        out_shape=(result,) * 6,
        in_specs=[in_hbm] * 6,
        out_specs=(in_vmem,) * 6,
        scratch_shapes=[
            pltpu.VMEM((2, half), BF16),
            pltpu.VMEM((1, channels), F32),
            pltpu.VMEM((n + 1, 1, chunk), F32),
            message,
            message,
            pltpu.VMEM((n * SUB, chunk), BF16),
            pltpu.VMEM((half, half + n * chunk), BF16),
            pltpu.VMEM((n * SUB, chunk), F32),
            message,
            message,
            pltpu.SemaphoreType.DMA((6,)),
            pltpu.SemaphoreType.DMA,
            pltpu.SemaphoreType.DMA((LINES,)),
            pltpu.SemaphoreType.DMA((2,)),
            pltpu.SemaphoreType.DMA((2,)),
            pltpu.SemaphoreType.DMA((2,)),
            pltpu.SemaphoreType.DMA((2,)),
        ],
        compiler_params=pltpu.CompilerParams(
            collective_id=0, has_side_effects=True, vmem_limit_bytes=32 * 1024 * 1024
        ),
    )(*[
        pltpu.with_memory_space_constraint(x, pltpu.HBM)
        for x in (first_gate, second_gate, values_in, cotangent, taps, skip_gain.reshape(1, channels))
    ])
    mixed_total = mixed_total.astype(F32)
    grad_mixed = grad_mixed.astype(F32)
    output = (values_in.astype(F32) * mixed_total).astype(BF16)
    grad_first = (grad_mixed * second_gate.astype(F32)).astype(BF16)
    grad_second = (grad_mixed * first_gate.astype(F32)).astype(BF16)
    grad_values = (cotangent.astype(F32) * mixed_total).astype(BF16)
    return (output, grad_first, grad_second, grad_values)


def solution(mesh):
    rows = P("seq", "ch")
    return jax.shard_map(
        functools.partial(on_device, mesh.shape["seq"]),
        mesh=mesh,
        in_specs=(rows, rows, rows, rows, P(("ch", "seq")), P("ch")),
        out_specs=(rows, rows, rows, rows),
        check_vma=False,
    )
```

```python
import functools

import jax
import jax.numpy as jnp
from jax import lax
from jax.experimental import pallas as pl
from jax.experimental.pallas import tpu as pltpu
from jax.sharding import PartitionSpec as P

BF16 = jnp.bfloat16
F32 = jnp.float32
SUB = 8
LINES = 4
NT = (((1,), (1,)), ((), ()))


def select_matrix(size, flipped):
    row = lax.broadcasted_iota(jnp.int32, (size, size), 0)
    col = lax.broadcasted_iota(jnp.int32, (size, size), 1)
    hit = (row + col == size - 1) if flipped else (row == col)
    return jnp.where(hit, 1.0, 0.0).astype(BF16)


def ring(step, size):
    return min(step, size - step)


def far_first(n):
    size = n // LINES
    steps = [(dx, dy) for dx in range(LINES) for dy in range(size)][1:]
    return sorted(steps, key=lambda s: (-ring(s[1], size), -ring(s[0], LINES), s))


def corner_first(n):
    size = n // LINES
    return sorted(range(n), key=lambda d: (ring(d % size, size) * 2 + ring(d // size, LINES) * 2 + (d % size > size // 2), d))


def kernel(
    n,
    fg_hbm, sg_hbm, vi_hbm, ct_hbm, taps_hbm, skip_hbm,
    fwd_ref, bwd_ref, fg, sg, vi, ct,
    tap_own, skip_own, tap_buf, send1, recv1, xbuf, slab, acc, send2, recv2,
    in_sem, tap_send, tap_recv, send1_sem, recv1_sem, send2_sem, recv2_sem,
):
    me = lax.axis_index("seq")
    half = fg_hbm.shape[0] // 2
    chunk = 2 * half
    channels = fg_hbm.shape[1]
    size = n // LINES
    line, place = me // size, lax.rem(me, size)

    def each_far_first(visit):
        for dx, dy in far_first(n):
            visit(lax.rem(line + dx, LINES) * size + lax.rem(place + dy, size))

    def each_corner_first(visit):
        for peer in corner_first(n):
            @pl.when(me != peer)
            def _(peer=peer):
                visit(peer)

    barrier = pltpu.get_barrier_semaphore()
    each_far_first(lambda peer: pl.semaphore_signal(barrier, inc=1, device_id={"seq": peer}))
    loads = [
        pltpu.make_async_copy(src, dst, in_sem.at[k])
        for k, (src, dst) in enumerate(
            ((taps_hbm, tap_own), (fg_hbm, fg), (sg_hbm, sg), (ct_hbm, ct), (vi_hbm, vi), (skip_hbm, skip_own))
        )
    ]
    for load in loads:
        load.start()

    tap_buf[0] = jnp.zeros((2, half), BF16)
    slab[:, 0:half] = jnp.zeros((half, half), BF16)
    loads[0].wait()
    tap_buf[me + 1] = tap_own[...]

    def messages(field):
        split = field.reshape(n, SUB, chunk)
        return jnp.concatenate([split[:, :, :half], split[:, :, half:]], axis=1).astype(BF16)

    plain = select_matrix(chunk, False)
    flipped = select_matrix(chunk, True)
    across = plain if channels == chunk else select_matrix(channels, False)
    loads[1].wait()
    loads[2].wait()
    gated = (fg[...].astype(F32) * sg[...].astype(F32)).astype(BF16)
    send1[0] = messages(lax.dot_general(across, gated, NT, preferred_element_type=F32))
    loads[3].wait()
    loads[4].wait()
    carried = (ct[...].astype(F32) * vi[...].astype(F32)).astype(BF16)
    carried = jnp.dot(flipped, carried, preferred_element_type=F32).astype(BF16)
    send1[1] = messages(lax.dot_general(across, carried, NT, preferred_element_type=F32))
    for way in range(2):
        recv1[way, me] = send1[way, me]

    lane = lax.broadcasted_iota(jnp.int32, (SUB, channels), 1)
    row = lax.broadcasted_iota(jnp.int32, (SUB, channels), 0)
    loads[5].wait()
    gains = jnp.sum(jnp.where(lane == me * SUB + row, skip_own[...], 0.0), axis=1, keepdims=True)

    pl.semaphore_wait(barrier, n - 1)

    def send_taps(peer):
        pltpu.make_async_remote_copy(
            src_ref=tap_buf.at[me + 1], dst_ref=tap_buf.at[me + 1],
            send_sem=tap_send, recv_sem=tap_recv.at[line], device_id={"seq": peer},
        ).start()

    def send_first(way, peer):
        pltpu.make_async_remote_copy(
            src_ref=send1.at[way, peer], dst_ref=recv1.at[way, me],
            send_sem=send1_sem.at[way], recv_sem=recv1_sem.at[way], device_id={"seq": peer},
        ).start()

    def send_second(way, peer):
        pltpu.make_async_remote_copy(
            src_ref=send2.at[way, peer], dst_ref=recv2.at[way, me],
            send_sem=send2_sem.at[way], recv_sem=recv2_sem.at[way], device_id={"seq": peer},
        ).start()

    def several(buf, count, send_sem, recv_sem):
        part = buf.at[pl.ds(0, count)]
        return pltpu.make_async_remote_copy(
            src_ref=part, dst_ref=part, send_sem=send_sem, recv_sem=recv_sem,
            device_id={"seq": lax.rem(me + 1, n)},
        )

    each_far_first(send_taps)
    for way in range(2):
        each_far_first(functools.partial(send_first, way))

    def build(j):
        before, here = tap_buf[j].astype(F32), tap_buf[j + 1].astype(F32)
        window = jnp.concatenate([before[1:2], here[0:1], here[1:2]], axis=1)
        window = jnp.broadcast_to(window, (half, half + chunk))
        skewed = pltpu.roll(window, 0, 1, stride=1, stride_axis=0)
        slab[:, pl.ds(pl.multiple_of(j * chunk + half, half), chunk)] = skewed[:, half:].astype(BF16)

    for dx in sorted(range(LINES), key=lambda dx: (ring(dx, LINES), dx)):
        source = lax.rem(line + dx, LINES)
        arrived = size - 1 if dx == 0 else size
        if arrived:
            several(tap_buf, arrived, tap_send, tap_recv.at[source]).wait_recv()
        for place_of in range(1, size):
            build(source * size + place_of)
    for source in range(LINES):
        build(source * size)

    for way in range(2):
        first = several(recv1.at[way], n - 1, send1_sem.at[way], recv1_sem.at[way])
        first.wait_recv()

        def block_of(block):
            source, side = (block, 0) if block < n else (2 * n - 1 - block, 1)
            return recv1[way, source].astype(F32)[side * SUB:(side + 1) * SUB]

        total = 2 * n * SUB
        previous = jnp.zeros((SUB, half), F32)
        for block in range(0, 2 * n, 2):
            here, later = block_of(block), block_of(block + 1)
            rows = slice(block * SUB, (block + 2) * SUB)
            xbuf[rows, :half] = jnp.concatenate([previous, here], axis=0).astype(BF16)
            xbuf[rows, half:] = jnp.concatenate([here, later], axis=0).astype(BF16)
            acc[block * SUB:(block + 1) * SUB] = gains * here
            acc[(block + 1) * SUB:(block + 2) * SUB] = gains * later
            previous = later

        for d in range(0, 2 * n, 4):
            lag = [slab[:, (d + e + 1) * half:(d + e + 2) * half] for e in range(4)]
            lags = jnp.concatenate(
                [jnp.concatenate([lag[1], lag[3]], axis=1), jnp.concatenate([lag[0], lag[2]], axis=1)], axis=0
            )
            depth = total - d * SUB
            term = jnp.dot(xbuf[0:depth, :], lags, preferred_element_type=F32)
            acc[d * SUB:total, :] = acc[d * SUB:total, :] + term[:, :half]
            acc[(d + 2) * SUB:total, :] = acc[(d + 2) * SUB:total, :] + term[:depth - 2 * SUB, half:]

        for dst in range(n):
            pieces = [acc[b * SUB:(b + 1) * SUB, :] for b in (dst, 2 * n - 1 - dst)]
            send2[way, dst] = jnp.concatenate(pieces, axis=0).astype(BF16)
        each_corner_first(functools.partial(send_second, way))
        recv2[way, me] = send2[way, me]

    for way, (out, matrix) in enumerate(((fwd_ref, plain), (bwd_ref, flipped))):
        second = several(recv2.at[way], n - 1, send2_sem.at[way], recv2_sem.at[way])
        second.wait_recv()
        back = recv2[way].astype(F32)
        left = back[:, :SUB].reshape(channels, half)
        right = back[:, SUB:].reshape(channels, half)
        back = jnp.concatenate([left, right], axis=1).astype(BF16)
        out[...] = lax.dot_general(matrix, back, NT, preferred_element_type=F32).astype(BF16)

    several(tap_buf, n - 1, tap_send, tap_recv.at[0]).wait_send()
    for way in range(2):
        several(recv1.at[way], n - 1, send1_sem.at[way], recv1_sem.at[way]).wait_send()
        several(recv2.at[way], n - 1, send2_sem.at[way], recv2_sem.at[way]).wait_send()


def on_device(n, first_gate, second_gate, values_in, cotangent, filters, skip_gain):
    chunk, channels = first_gate.shape
    half = chunk // 2
    taps = filters.reshape(2, half)
    in_hbm = pl.BlockSpec(memory_space=pltpu.HBM)
    in_vmem = pl.BlockSpec(memory_space=pltpu.VMEM)
    result = pltpu.VMEM((chunk, channels), BF16)
    message = pltpu.VMEM((2, n, 2 * SUB, half), BF16)
    mixed_total, grad_mixed, first_gate, second_gate, values_in, cotangent = pl.pallas_call(
        functools.partial(kernel, n),
        out_shape=(result,) * 6,
        in_specs=[in_hbm] * 6,
        out_specs=(in_vmem,) * 6,
        scratch_shapes=[
            pltpu.VMEM((2, half), BF16),
            pltpu.VMEM((1, channels), F32),
            pltpu.VMEM((n + 1, 2, half), BF16),
            message,
            message,
            pltpu.VMEM((2 * n * SUB, chunk), BF16),
            pltpu.VMEM((half, half + n * chunk), BF16),
            pltpu.VMEM((2 * n * SUB, half), F32),
            message,
            message,
            pltpu.SemaphoreType.DMA((6,)),
            pltpu.SemaphoreType.DMA,
            pltpu.SemaphoreType.DMA((LINES,)),
            pltpu.SemaphoreType.DMA((2,)),
            pltpu.SemaphoreType.DMA((2,)),
            pltpu.SemaphoreType.DMA((2,)),
            pltpu.SemaphoreType.DMA((2,)),
        ],
        compiler_params=pltpu.CompilerParams(
            collective_id=0, has_side_effects=True, vmem_limit_bytes=32 * 1024 * 1024
        ),
    )(*[
        pltpu.with_memory_space_constraint(x, pltpu.HBM)
        for x in (first_gate, second_gate, values_in, cotangent, taps, skip_gain.reshape(1, channels))
    ])
    mixed_total = mixed_total.astype(F32)
    grad_mixed = grad_mixed.astype(F32)
    output = (values_in.astype(F32) * mixed_total).astype(BF16)
    grad_first = (grad_mixed * second_gate.astype(F32)).astype(BF16)
    grad_second = (grad_mixed * first_gate.astype(F32)).astype(BF16)
    grad_values = (cotangent.astype(F32) * mixed_total).astype(BF16)
    return (output, grad_first, grad_second, grad_values)


def solution(mesh):
    rows = P("seq", "ch")
    return jax.shard_map(
        functools.partial(on_device, mesh.shape["seq"]),
        mesh=mesh,
        in_specs=(rows, rows, rows, rows, P(("ch", "seq")), P("ch")),
        out_specs=(rows, rows, rows, rows),
        check_vma=False,
    )
```

```python
import functools

import jax
import jax.numpy as jnp
from jax import lax
from jax.experimental import pallas as pl
from jax.experimental.pallas import tpu as pltpu
from jax.sharding import PartitionSpec as P

BF16 = jnp.bfloat16
F32 = jnp.float32
SUB = 8
LINES = 4
NT = (((1,), (1,)), ((), ()))


def select_matrix(size, flipped):
    row = lax.broadcasted_iota(jnp.int32, (size, size), 0)
    col = lax.broadcasted_iota(jnp.int32, (size, size), 1)
    hit = (row + col == size - 1) if flipped else (row == col)
    return jnp.where(hit, 1.0, 0.0).astype(BF16)


def ring(step, size):
    return min(step, size - step)


def far_first(n):
    size = n // LINES
    steps = [(dx, dy) for dx in range(LINES) for dy in range(size)][1:]
    return sorted(steps, key=lambda s: (-ring(s[1], size), -ring(s[0], LINES), s))


def corner_first(n):
    size = n // LINES
    return sorted(range(n), key=lambda d: (ring(d % size, size) * 2 + ring(d // size, LINES) * 2 + (d % size > size // 2), d))


def rows_of(messages):
    n, _, half = messages.shape
    back = messages[...].astype(F32)
    left = back[:, :SUB].reshape(n * SUB, half)
    right = back[:, SUB:].reshape(n * SUB, half)
    return jnp.concatenate([left, right], axis=1).astype(BF16)


def finish(mixed_ref, back_ref, fg, sg, vi, ct, out, grad_first, grad_second, grad_values, result, sem):
    def put(k, value, target):
        result[k] = value.astype(BF16)
        copy = pltpu.make_async_copy(result.at[k], target, sem.at[k])
        copy.start()
        return copy

    mixed = mixed_ref[...].astype(F32)
    copies = [put(0, vi[...].astype(F32) * mixed, out), put(3, ct[...].astype(F32) * mixed, grad_values)]
    flipped = select_matrix(fg.shape[0], True)
    grad = lax.dot_general(flipped, rows_of(back_ref), NT, preferred_element_type=F32)
    copies += [put(1, grad * sg[...].astype(F32), grad_first), put(2, grad * fg[...].astype(F32), grad_second)]
    for copy in copies:
        copy.wait()


def kernel(
    n,
    fg_hbm, sg_hbm, vi_hbm, ct_hbm, taps_hbm, skip_hbm,
    fwd_ref, recv2_bwd, fg, sg, vi, ct,
    tap_own, skip_own, tap_buf, send1, recv1, xbuf, slab, acc, send2, recv2_fwd,
    in_sem, tap_send, tap_recv, send1_sem, recv1_sem, send2_sem, recv2_sem,
):
    me = lax.axis_index("seq")
    half = fg_hbm.shape[0] // 2
    chunk = 2 * half
    channels = fg_hbm.shape[1]
    size = n // LINES
    line, place = me // size, lax.rem(me, size)

    def each_far_first(visit):
        for dx, dy in far_first(n):
            visit(lax.rem(line + dx, LINES) * size + lax.rem(place + dy, size))

    def each_corner_first(visit):
        for peer in corner_first(n):
            @pl.when(me != peer)
            def _(peer=peer):
                visit(peer)

    barrier = pltpu.get_barrier_semaphore()
    each_far_first(lambda peer: pl.semaphore_signal(barrier, inc=1, device_id={"seq": peer}))
    loads = [
        pltpu.make_async_copy(src, dst, in_sem.at[k])
        for k, (src, dst) in enumerate(
            ((taps_hbm, tap_own), (fg_hbm, fg), (sg_hbm, sg), (ct_hbm, ct), (vi_hbm, vi), (skip_hbm, skip_own))
        )
    ]
    for load in loads:
        load.start()

    tap_buf[0] = jnp.zeros((2, half), BF16)
    slab[:, 0:half] = jnp.zeros((half, half), BF16)
    loads[0].wait()
    tap_buf[me + 1] = tap_own[...]

    def messages(field):
        split = field.reshape(n, SUB, chunk)
        return jnp.concatenate([split[:, :, :half], split[:, :, half:]], axis=1).astype(BF16)

    plain = select_matrix(chunk, False)
    flipped = select_matrix(chunk, True)
    across = plain if channels == chunk else select_matrix(channels, False)
    loads[1].wait()
    loads[2].wait()
    gated = (fg[...].astype(F32) * sg[...].astype(F32)).astype(BF16)
    send1[0] = messages(lax.dot_general(across, gated, NT, preferred_element_type=F32))
    loads[3].wait()
    loads[4].wait()
    carried = (ct[...].astype(F32) * vi[...].astype(F32)).astype(BF16)
    carried = jnp.dot(flipped, carried, preferred_element_type=F32).astype(BF16)
    send1[1] = messages(lax.dot_general(across, carried, NT, preferred_element_type=F32))
    for way in range(2):
        recv1[way, me] = send1[way, me]

    lane = lax.broadcasted_iota(jnp.int32, (SUB, channels), 1)
    row = lax.broadcasted_iota(jnp.int32, (SUB, channels), 0)
    loads[5].wait()
    gains = jnp.sum(jnp.where(lane == me * SUB + row, skip_own[...], 0.0), axis=1, keepdims=True)

    pl.semaphore_wait(barrier, n - 1)

    def send_taps(peer):
        pltpu.make_async_remote_copy(
            src_ref=tap_buf.at[me + 1], dst_ref=tap_buf.at[me + 1],
            send_sem=tap_send, recv_sem=tap_recv.at[line], device_id={"seq": peer},
        ).start()

    def send_first(way, peer):
        pltpu.make_async_remote_copy(
            src_ref=send1.at[way, peer], dst_ref=recv1.at[way, me],
            send_sem=send1_sem.at[way], recv_sem=recv1_sem.at[way], device_id={"seq": peer},
        ).start()

    recv2 = (recv2_fwd, recv2_bwd)

    def send_second(way, peer):
        pltpu.make_async_remote_copy(
            src_ref=send2.at[way, peer], dst_ref=recv2[way].at[me],
            send_sem=send2_sem.at[way], recv_sem=recv2_sem.at[way], device_id={"seq": peer},
        ).start()

    def several(buf, count, send_sem, recv_sem):
        part = buf.at[pl.ds(0, count)]
        return pltpu.make_async_remote_copy(
            src_ref=part, dst_ref=part, send_sem=send_sem, recv_sem=recv_sem,
            device_id={"seq": lax.rem(me + 1, n)},
        )

    each_far_first(send_taps)
    for way in range(2):
        each_far_first(functools.partial(send_first, way))

    def build(j):
        before, here = tap_buf[j].astype(F32), tap_buf[j + 1].astype(F32)
        window = jnp.concatenate([before[1:2], here[0:1], here[1:2]], axis=1)
        window = jnp.broadcast_to(window, (half, half + chunk))
        skewed = pltpu.roll(window, 0, 1, stride=1, stride_axis=0)
        slab[:, pl.ds(pl.multiple_of(j * chunk + half, half), chunk)] = skewed[:, half:].astype(BF16)

    for dx in sorted(range(LINES), key=lambda dx: (ring(dx, LINES), dx)):
        source = lax.rem(line + dx, LINES)
        arrived = size - 1 if dx == 0 else size
        if arrived:
            several(tap_buf, arrived, tap_send, tap_recv.at[source]).wait_recv()
        for place_of in range(1, size):
            build(source * size + place_of)
    for source in range(LINES):
        build(source * size)

    for way in range(2):
        first = several(recv1.at[way], n - 1, send1_sem.at[way], recv1_sem.at[way])
        first.wait_recv()

        def block_of(block):
            source, side = (block, 0) if block < n else (2 * n - 1 - block, 1)
            return recv1[way, source].astype(F32)[side * SUB:(side + 1) * SUB]

        total = 2 * n * SUB
        previous = jnp.zeros((SUB, half), F32)
        for block in range(0, 2 * n, 2):
            here, later = block_of(block), block_of(block + 1)
            rows = slice(block * SUB, (block + 2) * SUB)
            xbuf[rows, :half] = jnp.concatenate([previous, here], axis=0).astype(BF16)
            xbuf[rows, half:] = jnp.concatenate([here, later], axis=0).astype(BF16)
            acc[block * SUB:(block + 1) * SUB] = gains * here
            acc[(block + 1) * SUB:(block + 2) * SUB] = gains * later
            previous = later

        for d in range(0, 2 * n, 4):
            lag = [slab[:, (d + e + 1) * half:(d + e + 2) * half] for e in range(4)]
            lags = jnp.concatenate(
                [jnp.concatenate([lag[1], lag[3]], axis=1), jnp.concatenate([lag[0], lag[2]], axis=1)], axis=0
            )
            depth = total - d * SUB
            term = jnp.dot(xbuf[0:depth, :], lags, preferred_element_type=F32)
            acc[d * SUB:total, :] = acc[d * SUB:total, :] + term[:, :half]
            acc[(d + 2) * SUB:total, :] = acc[(d + 2) * SUB:total, :] + term[:depth - 2 * SUB, half:]

        for dst in range(n):
            pieces = [acc[b * SUB:(b + 1) * SUB, :] for b in (dst, 2 * n - 1 - dst)]
            send2[way, dst] = jnp.concatenate(pieces, axis=0).astype(BF16)
        each_corner_first(functools.partial(send_second, way))
        recv2[way][me] = send2[way, me]

    several(recv2_fwd, n - 1, send2_sem.at[0], recv2_sem.at[0]).wait_recv()
    fwd_ref[...] = lax.dot_general(plain, rows_of(recv2_fwd), NT, preferred_element_type=F32).astype(BF16)
    several(recv2_bwd, n - 1, send2_sem.at[1], recv2_sem.at[1]).wait_recv()

    several(tap_buf, n - 1, tap_send, tap_recv.at[0]).wait_send()
    for way in range(2):
        several(recv1.at[way], n - 1, send1_sem.at[way], recv1_sem.at[way]).wait_send()
        several(recv2[way], n - 1, send2_sem.at[way], recv2_sem.at[way]).wait_send()


def on_device(n, first_gate, second_gate, values_in, cotangent, filters, skip_gain):
    chunk, channels = first_gate.shape
    half = chunk // 2
    taps = filters.reshape(2, half)
    in_hbm = pl.BlockSpec(memory_space=pltpu.HBM)
    in_vmem = pl.BlockSpec(memory_space=pltpu.VMEM)
    result = pltpu.VMEM((chunk, channels), BF16)
    message = pltpu.VMEM((2, n, 2 * SUB, half), BF16)
    mixed, back, *gates = pl.pallas_call(
        functools.partial(kernel, n),
        out_shape=(result, pltpu.VMEM((n, 2 * SUB, half), BF16)) + (result,) * 4,
        in_specs=[in_hbm] * 6,
        out_specs=(in_vmem,) * 6,
        scratch_shapes=[
            pltpu.VMEM((2, half), BF16),
            pltpu.VMEM((1, channels), F32),
            pltpu.VMEM((n + 1, 2, half), BF16),
            message,
            message,
            pltpu.VMEM((2 * n * SUB, chunk), BF16),
            pltpu.VMEM((half, half + n * chunk), BF16),
            pltpu.VMEM((2 * n * SUB, half), F32),
            message,
            pltpu.VMEM((n, 2 * SUB, half), BF16),
            pltpu.SemaphoreType.DMA((6,)),
            pltpu.SemaphoreType.DMA,
            pltpu.SemaphoreType.DMA((LINES,)),
            pltpu.SemaphoreType.DMA((2,)),
            pltpu.SemaphoreType.DMA((2,)),
            pltpu.SemaphoreType.DMA((2,)),
            pltpu.SemaphoreType.DMA((2,)),
        ],
        compiler_params=pltpu.CompilerParams(
            collective_id=0, has_side_effects=True, vmem_limit_bytes=32 * 1024 * 1024
        ),
    )(*[
        pltpu.with_memory_space_constraint(x, pltpu.HBM)
        for x in (first_gate, second_gate, values_in, cotangent, taps, skip_gain.reshape(1, channels))
    ])
    return pl.pallas_call(
        finish,
        out_shape=(jax.ShapeDtypeStruct((chunk, channels), BF16),) * 4,
        in_specs=[in_vmem] * 6,
        out_specs=(in_hbm,) * 4,
        scratch_shapes=[pltpu.VMEM((4, chunk, channels), BF16), pltpu.SemaphoreType.DMA((4,))],
        compiler_params=pltpu.CompilerParams(vmem_limit_bytes=16 * 1024 * 1024),
    )(*[pltpu.with_memory_space_constraint(x, pltpu.VMEM) for x in (mixed, back, *gates)])


def solution(mesh):
    rows = P("seq", "ch")
    return jax.shard_map(
        functools.partial(on_device, mesh.shape["seq"]),
        mesh=mesh,
        in_specs=(rows, rows, rows, rows, P(("ch", "seq")), P("ch")),
        out_specs=(rows, rows, rows, rows),
        check_vma=False,
    )
```

```python
import functools

import jax
import jax.numpy as jnp
from jax import lax
from jax.experimental import pallas as pl
from jax.experimental.pallas import tpu as pltpu
from jax.sharding import PartitionSpec as P

BF16 = jnp.bfloat16
F32 = jnp.float32
SUB = 8
LINES = 4
NT = (((1,), (1,)), ((), ()))


def select_matrix(size, flipped):
    row = lax.broadcasted_iota(jnp.int32, (size, size), 0)
    col = lax.broadcasted_iota(jnp.int32, (size, size), 1)
    hit = (row + col == size - 1) if flipped else (row == col)
    return jnp.where(hit, 1.0, 0.0).astype(BF16)


def ring(step, size):
    return min(step, size - step)


def far_first(n):
    size = n // LINES
    steps = [(dx, dy) for dx in range(LINES) for dy in range(size)][1:]
    return sorted(steps, key=lambda s: (-ring(s[1], size), -ring(s[0], LINES), s))


def corner_first(n):
    size = n // LINES
    return sorted(range(n), key=lambda d: (ring(d % size, size) * 2 + ring(d // size, LINES) * 2 + (d % size > size // 2), d))


def rows_of(messages):
    n, _, half = messages.shape
    back = messages[...].astype(F32)
    left = back[:, :SUB].reshape(n * SUB, half)
    right = back[:, SUB:].reshape(n * SUB, half)
    return jnp.concatenate([left, right], axis=1).astype(BF16)


def finish(mixed_ref, back_ref, flip, fg, sg, vi, ct, out, grad_first, grad_second, grad_values, result, sem):
    def put(k, value, target):
        result[k] = value.astype(BF16)
        copy = pltpu.make_async_copy(result.at[k], target, sem.at[k])
        copy.start()
        return copy

    mixed = mixed_ref[...].astype(F32)
    copies = [put(0, vi[...].astype(F32) * mixed, out), put(3, ct[...].astype(F32) * mixed, grad_values)]
    grad = lax.dot_general(flip[...], rows_of(back_ref), NT, preferred_element_type=F32)
    copies += [put(1, grad * sg[...].astype(F32), grad_first), put(2, grad * fg[...].astype(F32), grad_second)]
    for copy in copies:
        copy.wait()


def kernel(
    n,
    fg_hbm, sg_hbm, vi_hbm, ct_hbm, taps_hbm, skip_hbm,
    fwd_ref, recv2_bwd, flip, fg, sg, vi, ct,
    tap_own, skip_own, tap_buf, send1, recv1, xbuf, slab, acc, send2, recv2_fwd,
    in_sem, tap_send, tap_recv, send1_sem, recv1_sem, send2_sem, recv2_sem,
):
    me = lax.axis_index("seq")
    half = fg_hbm.shape[0] // 2
    chunk = 2 * half
    channels = fg_hbm.shape[1]
    size = n // LINES
    line, place = me // size, lax.rem(me, size)

    def each_far_first(visit):
        for dx, dy in far_first(n):
            visit(lax.rem(line + dx, LINES) * size + lax.rem(place + dy, size))

    def each_corner_first(visit):
        for peer in corner_first(n):
            @pl.when(me != peer)
            def _(peer=peer):
                visit(peer)

    barrier = pltpu.get_barrier_semaphore()
    each_far_first(lambda peer: pl.semaphore_signal(barrier, inc=1, device_id={"seq": peer}))
    loads = [
        pltpu.make_async_copy(src, dst, in_sem.at[k])
        for k, (src, dst) in enumerate(
            ((taps_hbm, tap_own), (fg_hbm, fg), (sg_hbm, sg), (ct_hbm, ct), (vi_hbm, vi), (skip_hbm, skip_own))
        )
    ]
    for load in loads:
        load.start()

    tap_buf[0] = jnp.zeros((2, half), BF16)
    slab[:, 0:half] = jnp.zeros((half, half), BF16)
    loads[0].wait()
    tap_buf[me + 1] = tap_own[...]

    def messages(field):
        split = field.reshape(n, SUB, chunk)
        return jnp.concatenate([split[:, :, :half], split[:, :, half:]], axis=1).astype(BF16)

    plain = select_matrix(chunk, False)
    flipped = select_matrix(chunk, True)
    flip[...] = flipped
    across = plain if channels == chunk else select_matrix(channels, False)
    loads[1].wait()
    loads[2].wait()
    gated = (fg[...].astype(F32) * sg[...].astype(F32)).astype(BF16)
    send1[0] = messages(lax.dot_general(across, gated, NT, preferred_element_type=F32))
    loads[3].wait()
    loads[4].wait()
    carried = (ct[...].astype(F32) * vi[...].astype(F32)).astype(BF16)
    carried = jnp.dot(flipped, carried, preferred_element_type=F32).astype(BF16)
    send1[1] = messages(lax.dot_general(across, carried, NT, preferred_element_type=F32))
    for way in range(2):
        recv1[way, me] = send1[way, me]

    lane = lax.broadcasted_iota(jnp.int32, (SUB, channels), 1)
    row = lax.broadcasted_iota(jnp.int32, (SUB, channels), 0)
    loads[5].wait()
    gains = jnp.sum(jnp.where(lane == me * SUB + row, skip_own[...], 0.0), axis=1, keepdims=True)

    pl.semaphore_wait(barrier, n - 1)

    def send_taps(peer):
        pltpu.make_async_remote_copy(
            src_ref=tap_buf.at[me + 1], dst_ref=tap_buf.at[me + 1],
            send_sem=tap_send, recv_sem=tap_recv.at[line], device_id={"seq": peer},
        ).start()

    def send_first(way, peer):
        pltpu.make_async_remote_copy(
            src_ref=send1.at[way, peer], dst_ref=recv1.at[way, me],
            send_sem=send1_sem.at[way], recv_sem=recv1_sem.at[way], device_id={"seq": peer},
        ).start()

    recv2 = (recv2_fwd, recv2_bwd)

    def send_second(way, peer):
        pltpu.make_async_remote_copy(
            src_ref=send2.at[way, peer], dst_ref=recv2[way].at[me],
            send_sem=send2_sem.at[way], recv_sem=recv2_sem.at[way], device_id={"seq": peer},
        ).start()

    def several(buf, count, send_sem, recv_sem):
        part = buf.at[pl.ds(0, count)]
        return pltpu.make_async_remote_copy(
            src_ref=part, dst_ref=part, send_sem=send_sem, recv_sem=recv_sem,
            device_id={"seq": lax.rem(me + 1, n)},
        )

    patient = lax.rem(lax.axis_index("ch"), 2) == 1
    each_far_first(send_taps)
    each_far_first(functools.partial(send_first, 0))

    @pl.when(jnp.logical_not(patient))
    def _():
        each_far_first(functools.partial(send_first, 1))

    def build(j):
        before, here = tap_buf[j].astype(F32), tap_buf[j + 1].astype(F32)
        window = jnp.concatenate([before[1:2], here[0:1], here[1:2]], axis=1)
        window = jnp.broadcast_to(window, (half, half + chunk))
        skewed = pltpu.roll(window, 0, 1, stride=1, stride_axis=0)
        slab[:, pl.ds(pl.multiple_of(j * chunk + half, half), chunk)] = skewed[:, half:].astype(BF16)

    here = []
    for dx in sorted(range(LINES), key=lambda dx: (ring(dx, LINES), dx)):
        source = lax.rem(line + dx, LINES)
        arrived = size - 1 if dx == 0 else size
        if arrived:
            several(tap_buf, arrived, tap_send, tap_recv.at[source]).wait_recv()
        here.append(dx)
        for place_of in range(1, size):
            build(source * size + place_of)
        if len(here) == 2:
            @pl.when(patient)
            def _():
                each_far_first(functools.partial(send_first, 1))

        for first in (dx, (dx + 1) % LINES):
            if first in here and (first - 1) % LINES in here:
                build(lax.rem(line + first, LINES) * size)

    for way in range(2):
        first = several(recv1.at[way], n - 1, send1_sem.at[way], recv1_sem.at[way])
        first.wait_recv()

        def block_of(block):
            source, side = (block, 0) if block < n else (2 * n - 1 - block, 1)
            return recv1[way, source].astype(F32)[side * SUB:(side + 1) * SUB]

        total = 2 * n * SUB
        previous = jnp.zeros((SUB, half), F32)
        for block in range(0, 2 * n, 2):
            here, later = block_of(block), block_of(block + 1)
            rows = slice(block * SUB, (block + 2) * SUB)
            xbuf[rows, :half] = jnp.concatenate([previous, here], axis=0).astype(BF16)
            xbuf[rows, half:] = jnp.concatenate([here, later], axis=0).astype(BF16)
            acc[block * SUB:(block + 1) * SUB] = gains * here
            acc[(block + 1) * SUB:(block + 2) * SUB] = gains * later
            previous = later

        for d in range(0, 2 * n, 4):
            lag = [slab[:, (d + e + 1) * half:(d + e + 2) * half] for e in range(4)]
            lags = jnp.concatenate(
                [jnp.concatenate([lag[1], lag[3]], axis=1), jnp.concatenate([lag[0], lag[2]], axis=1)], axis=0
            )
            depth = total - d * SUB
            term = jnp.dot(xbuf[0:depth, :], lags, preferred_element_type=F32)
            acc[d * SUB:total, :] = acc[d * SUB:total, :] + term[:, :half]
            acc[(d + 2) * SUB:total, :] = acc[(d + 2) * SUB:total, :] + term[:depth - 2 * SUB, half:]

        for dst in range(n):
            pieces = [acc[b * SUB:(b + 1) * SUB, :] for b in (dst, 2 * n - 1 - dst)]
            send2[way, dst] = jnp.concatenate(pieces, axis=0).astype(BF16)
        each_corner_first(functools.partial(send_second, way))
        recv2[way][me] = send2[way, me]

    several(recv2_fwd, n - 1, send2_sem.at[0], recv2_sem.at[0]).wait_recv()
    fwd_ref[...] = lax.dot_general(plain, rows_of(recv2_fwd), NT, preferred_element_type=F32).astype(BF16)
    several(recv2_bwd, n - 1, send2_sem.at[1], recv2_sem.at[1]).wait_recv()

    several(tap_buf, n - 1, tap_send, tap_recv.at[0]).wait_send()
    for way in range(2):
        several(recv1.at[way], n - 1, send1_sem.at[way], recv1_sem.at[way]).wait_send()
        several(recv2[way], n - 1, send2_sem.at[way], recv2_sem.at[way]).wait_send()


def on_device(n, first_gate, second_gate, values_in, cotangent, filters, skip_gain):
    chunk, channels = first_gate.shape
    half = chunk // 2
    taps = filters.reshape(2, half)
    in_hbm = pl.BlockSpec(memory_space=pltpu.HBM)
    in_vmem = pl.BlockSpec(memory_space=pltpu.VMEM)
    result = pltpu.VMEM((chunk, channels), BF16)
    message = pltpu.VMEM((2, n, 2 * SUB, half), BF16)
    mixed, back, flip, *gates = pl.pallas_call(
        functools.partial(kernel, n),
        out_shape=(result, pltpu.VMEM((n, 2 * SUB, half), BF16), pltpu.VMEM((chunk, chunk), BF16)) + (result,) * 4,
        in_specs=[in_hbm] * 6,
        out_specs=(in_vmem,) * 7,
        scratch_shapes=[
            pltpu.VMEM((2, half), BF16),
            pltpu.VMEM((1, channels), F32),
            pltpu.VMEM((n + 1, 2, half), BF16),
            message,
            message,
            pltpu.VMEM((2 * n * SUB, chunk), BF16),
            pltpu.VMEM((half, half + n * chunk), BF16),
            pltpu.VMEM((2 * n * SUB, half), F32),
            message,
            pltpu.VMEM((n, 2 * SUB, half), BF16),
            pltpu.SemaphoreType.DMA((6,)),
            pltpu.SemaphoreType.DMA,
            pltpu.SemaphoreType.DMA((LINES,)),
            pltpu.SemaphoreType.DMA((2,)),
            pltpu.SemaphoreType.DMA((2,)),
            pltpu.SemaphoreType.DMA((2,)),
            pltpu.SemaphoreType.DMA((2,)),
        ],
        compiler_params=pltpu.CompilerParams(
            collective_id=0, has_side_effects=True, vmem_limit_bytes=32 * 1024 * 1024
        ),
    )(*[
        pltpu.with_memory_space_constraint(x, pltpu.HBM)
        for x in (first_gate, second_gate, values_in, cotangent, taps, skip_gain.reshape(1, channels))
    ])
    return pl.pallas_call(
        finish,
        out_shape=(jax.ShapeDtypeStruct((chunk, channels), BF16),) * 4,
        in_specs=[in_vmem] * 7,
        out_specs=(in_hbm,) * 4,
        scratch_shapes=[pltpu.VMEM((4, chunk, channels), BF16), pltpu.SemaphoreType.DMA((4,))],
        compiler_params=pltpu.CompilerParams(vmem_limit_bytes=16 * 1024 * 1024),
    )(*[pltpu.with_memory_space_constraint(x, pltpu.VMEM) for x in (mixed, back, flip, *gates)])


def solution(mesh):
    rows = P("seq", "ch")
    return jax.shard_map(
        functools.partial(on_device, mesh.shape["seq"]),
        mesh=mesh,
        in_specs=(rows, rows, rows, rows, P(("ch", "seq")), P("ch")),
        out_specs=(rows, rows, rows, rows),
        check_vma=False,
    )
```

```python
import functools

import jax
import jax.numpy as jnp
from jax import lax
from jax.experimental import pallas as pl
from jax.experimental.pallas import tpu as pltpu
from jax.sharding import PartitionSpec as P

BF16 = jnp.bfloat16
F32 = jnp.float32
SUB = 8
LINES = 4
NT = (((1,), (1,)), ((), ()))


def select_matrix(size, flipped):
    row = lax.broadcasted_iota(jnp.int32, (size, size), 0)
    col = lax.broadcasted_iota(jnp.int32, (size, size), 1)
    hit = (row + col == size - 1) if flipped else (row == col)
    return jnp.where(hit, 1.0, 0.0).astype(BF16)


def ring(step, size):
    return min(step, size - step)


def far_first(n):
    size = n // LINES
    steps = [(dx, dy) for dx in range(LINES) for dy in range(size)][1:]
    return sorted(steps, key=lambda s: (-ring(s[1], size) - ring(s[0], LINES), s))


def corner_first(n):
    size = n // LINES
    return sorted(range(n), key=lambda d: (ring(d % size, size) * 2 + ring(d // size, LINES) * 2 + (d % size > size // 2), d))


def rows_of(messages):
    n, _, half = messages.shape
    back = messages[...].astype(F32)
    left = back[:, :SUB].reshape(n * SUB, half)
    right = back[:, SUB:].reshape(n * SUB, half)
    return jnp.concatenate([left, right], axis=1).astype(BF16)


def finish(mixed_ref, back_ref, flip, fg, sg, vi, ct, out, grad_first, grad_second, grad_values, result, sem):
    def put(k, value, target):
        result[k] = value.astype(BF16)
        copy = pltpu.make_async_copy(result.at[k], target, sem.at[k])
        copy.start()
        return copy

    mixed = mixed_ref[...].astype(F32)
    copies = [put(0, vi[...].astype(F32) * mixed, out), put(3, ct[...].astype(F32) * mixed, grad_values)]
    grad = lax.dot_general(flip[...], rows_of(back_ref), NT, preferred_element_type=F32)
    copies += [put(1, grad * sg[...].astype(F32), grad_first), put(2, grad * fg[...].astype(F32), grad_second)]
    for copy in copies:
        copy.wait()


def kernel(
    n,
    fg_hbm, sg_hbm, vi_hbm, ct_hbm, taps_hbm, skip_hbm,
    fwd_ref, recv2_bwd, flip, fg, sg, vi, ct,
    tap_own, skip_own, tap_buf, send1, recv1, xbuf, slab, acc, send2, recv2_fwd,
    in_sem, tap_send, tap_recv, send1_sem, recv1_sem, send2_sem, recv2_sem,
):
    me = lax.axis_index("seq")
    half = fg_hbm.shape[0] // 2
    chunk = 2 * half
    channels = fg_hbm.shape[1]
    size = n // LINES
    line, place = me // size, lax.rem(me, size)

    def each_far_first(visit):
        for dx, dy in far_first(n):
            visit(lax.rem(line + dx, LINES) * size + lax.rem(place + dy, size))

    def each_corner_first(visit):
        for peer in corner_first(n):
            @pl.when(me != peer)
            def _(peer=peer):
                visit(peer)

    barrier = pltpu.get_barrier_semaphore()
    each_far_first(lambda peer: pl.semaphore_signal(barrier, inc=1, device_id={"seq": peer}))
    loads = [
        pltpu.make_async_copy(src, dst, in_sem.at[k])
        for k, (src, dst) in enumerate(
            ((taps_hbm, tap_own), (fg_hbm, fg), (sg_hbm, sg), (ct_hbm, ct), (vi_hbm, vi), (skip_hbm, skip_own))
        )
    ]
    for load in loads:
        load.start()

    tap_buf[0] = jnp.zeros((2, half), BF16)
    slab[:, 0:half] = jnp.zeros((half, half), BF16)
    loads[0].wait()
    tap_buf[me + 1] = tap_own[...]

    def messages(field):
        split = field.reshape(n, SUB, chunk)
        return jnp.concatenate([split[:, :, :half], split[:, :, half:]], axis=1).astype(BF16)

    plain = select_matrix(chunk, False)
    flipped = select_matrix(chunk, True)
    flip[...] = flipped
    across = plain if channels == chunk else select_matrix(channels, False)
    loads[1].wait()
    loads[2].wait()
    gated = (fg[...].astype(F32) * sg[...].astype(F32)).astype(BF16)
    send1[0] = messages(lax.dot_general(across, gated, NT, preferred_element_type=F32))
    loads[3].wait()
    loads[4].wait()
    carried = (ct[...].astype(F32) * vi[...].astype(F32)).astype(BF16)
    carried = jnp.dot(flipped, carried, preferred_element_type=F32).astype(BF16)
    send1[1] = messages(lax.dot_general(across, carried, NT, preferred_element_type=F32))
    for way in range(2):
        recv1[way, me] = send1[way, me]

    lane = lax.broadcasted_iota(jnp.int32, (SUB, channels), 1)
    row = lax.broadcasted_iota(jnp.int32, (SUB, channels), 0)
    loads[5].wait()
    gains = jnp.sum(jnp.where(lane == me * SUB + row, skip_own[...], 0.0), axis=1, keepdims=True)

    pl.semaphore_wait(barrier, n - 1)

    def send_taps(peer):
        pltpu.make_async_remote_copy(
            src_ref=tap_buf.at[me + 1], dst_ref=tap_buf.at[me + 1],
            send_sem=tap_send, recv_sem=tap_recv.at[line], device_id={"seq": peer},
        ).start()

    def send_first(way, peer):
        pltpu.make_async_remote_copy(
            src_ref=send1.at[way, peer], dst_ref=recv1.at[way, me],
            send_sem=send1_sem.at[way], recv_sem=recv1_sem.at[way], device_id={"seq": peer},
        ).start()

    recv2 = (recv2_fwd, recv2_bwd)

    def send_second(way, peer):
        pltpu.make_async_remote_copy(
            src_ref=send2.at[way, peer], dst_ref=recv2[way].at[me],
            send_sem=send2_sem.at[way], recv_sem=recv2_sem.at[way], device_id={"seq": peer},
        ).start()

    def several(buf, count, send_sem, recv_sem):
        part = buf.at[pl.ds(0, count)]
        return pltpu.make_async_remote_copy(
            src_ref=part, dst_ref=part, send_sem=send_sem, recv_sem=recv_sem,
            device_id={"seq": lax.rem(me + 1, n)},
        )

    patient = lax.rem(lax.axis_index("ch"), 2) == 1
    each_far_first(send_taps)
    each_far_first(functools.partial(send_first, 0))

    @pl.when(jnp.logical_not(patient))
    def _():
        each_far_first(functools.partial(send_first, 1))

    def build(j):
        before, here = tap_buf[j].astype(F32), tap_buf[j + 1].astype(F32)
        window = jnp.concatenate([before[1:2], here[0:1], here[1:2]], axis=1)
        window = jnp.broadcast_to(window, (half, half + chunk))
        skewed = pltpu.roll(window, 0, 1, stride=1, stride_axis=0)
        slab[:, pl.ds(pl.multiple_of(j * chunk + half, half), chunk)] = skewed[:, half:].astype(BF16)

    here = []
    for dx in sorted(range(LINES), key=lambda dx: (ring(dx, LINES), dx)):
        source = lax.rem(line + dx, LINES)
        arrived = size - 1 if dx == 0 else size
        if arrived:
            several(tap_buf, arrived, tap_send, tap_recv.at[source]).wait_recv()
        here.append(dx)
        for place_of in range(1, size):
            build(source * size + place_of)
        if len(here) == 2:
            @pl.when(patient)
            def _():
                each_far_first(functools.partial(send_first, 1))

        for first in (dx, (dx + 1) % LINES):
            if first in here and (first - 1) % LINES in here:
                build(lax.rem(line + first, LINES) * size)

    for way in range(2):
        first = several(recv1.at[way], n - 1, send1_sem.at[way], recv1_sem.at[way])
        first.wait_recv()

        def block_of(block):
            source, side = (block, 0) if block < n else (2 * n - 1 - block, 1)
            return recv1[way, source].astype(F32)[side * SUB:(side + 1) * SUB]

        total = 2 * n * SUB
        previous = jnp.zeros((SUB, half), F32)
        for block in range(0, 2 * n, 2):
            here, later = block_of(block), block_of(block + 1)
            rows = slice(block * SUB, (block + 2) * SUB)
            xbuf[rows, :half] = jnp.concatenate([previous, here], axis=0).astype(BF16)
            xbuf[rows, half:] = jnp.concatenate([here, later], axis=0).astype(BF16)
            acc[block * SUB:(block + 1) * SUB] = gains * here
            acc[(block + 1) * SUB:(block + 2) * SUB] = gains * later
            previous = later

        for d in range(0, 2 * n, 4):
            lag = [slab[:, (d + e + 1) * half:(d + e + 2) * half] for e in range(4)]
            lags = jnp.concatenate(
                [jnp.concatenate([lag[1], lag[3]], axis=1), jnp.concatenate([lag[0], lag[2]], axis=1)], axis=0
            )
            depth = total - d * SUB
            term = jnp.dot(xbuf[0:depth, :], lags, preferred_element_type=F32)
            acc[d * SUB:total, :] = acc[d * SUB:total, :] + term[:, :half]
            acc[(d + 2) * SUB:total, :] = acc[(d + 2) * SUB:total, :] + term[:depth - 2 * SUB, half:]

        for dst in range(n):
            pieces = [acc[b * SUB:(b + 1) * SUB, :] for b in (dst, 2 * n - 1 - dst)]
            send2[way, dst] = jnp.concatenate(pieces, axis=0).astype(BF16)
        each_corner_first(functools.partial(send_second, way))
        recv2[way][me] = send2[way, me]

    several(recv2_fwd, n - 1, send2_sem.at[0], recv2_sem.at[0]).wait_recv()
    fwd_ref[...] = lax.dot_general(plain, rows_of(recv2_fwd), NT, preferred_element_type=F32).astype(BF16)
    several(recv2_bwd, n - 1, send2_sem.at[1], recv2_sem.at[1]).wait_recv()

    several(tap_buf, n - 1, tap_send, tap_recv.at[0]).wait_send()
    for way in range(2):
        several(recv1.at[way], n - 1, send1_sem.at[way], recv1_sem.at[way]).wait_send()
        several(recv2[way], n - 1, send2_sem.at[way], recv2_sem.at[way]).wait_send()


def on_device(n, first_gate, second_gate, values_in, cotangent, filters, skip_gain):
    chunk, channels = first_gate.shape
    half = chunk // 2
    taps = filters.reshape(2, half)
    in_hbm = pl.BlockSpec(memory_space=pltpu.HBM)
    in_vmem = pl.BlockSpec(memory_space=pltpu.VMEM)
    result = pltpu.VMEM((chunk, channels), BF16)
    message = pltpu.VMEM((2, n, 2 * SUB, half), BF16)
    mixed, back, flip, *gates = pl.pallas_call(
        functools.partial(kernel, n),
        out_shape=(result, pltpu.VMEM((n, 2 * SUB, half), BF16), pltpu.VMEM((chunk, chunk), BF16)) + (result,) * 4,
        in_specs=[in_hbm] * 6,
        out_specs=(in_vmem,) * 7,
        scratch_shapes=[
            pltpu.VMEM((2, half), BF16),
            pltpu.VMEM((1, channels), F32),
            pltpu.VMEM((n + 1, 2, half), BF16),
            message,
            message,
            pltpu.VMEM((2 * n * SUB, chunk), BF16),
            pltpu.VMEM((half, half + n * chunk), BF16),
            pltpu.VMEM((2 * n * SUB, half), F32),
            message,
            pltpu.VMEM((n, 2 * SUB, half), BF16),
            pltpu.SemaphoreType.DMA((6,)),
            pltpu.SemaphoreType.DMA,
            pltpu.SemaphoreType.DMA((LINES,)),
            pltpu.SemaphoreType.DMA((2,)),
            pltpu.SemaphoreType.DMA((2,)),
            pltpu.SemaphoreType.DMA((2,)),
            pltpu.SemaphoreType.DMA((2,)),
        ],
        compiler_params=pltpu.CompilerParams(
            collective_id=0, has_side_effects=True, vmem_limit_bytes=32 * 1024 * 1024
        ),
    )(*[
        pltpu.with_memory_space_constraint(x, pltpu.HBM)
        for x in (first_gate, second_gate, values_in, cotangent, taps, skip_gain.reshape(1, channels))
    ])
    return pl.pallas_call(
        finish,
        out_shape=(jax.ShapeDtypeStruct((chunk, channels), BF16),) * 4,
        in_specs=[in_vmem] * 7,
        out_specs=(in_hbm,) * 4,
        scratch_shapes=[pltpu.VMEM((4, chunk, channels), BF16), pltpu.SemaphoreType.DMA((4,))],
        compiler_params=pltpu.CompilerParams(vmem_limit_bytes=16 * 1024 * 1024),
    )(*[pltpu.with_memory_space_constraint(x, pltpu.VMEM) for x in (mixed, back, flip, *gates)])


def solution(mesh):
    rows = P("seq", "ch")
    return jax.shard_map(
        functools.partial(on_device, mesh.shape["seq"]),
        mesh=mesh,
        in_specs=(rows, rows, rows, rows, P(("ch", "seq")), P("ch")),
        out_specs=(rows, rows, rows, rows),
        check_vma=False,
    )
```
